32 devices in a mesh: groups: 2 (over y), segment: 4 (over x, core), space: 4 (over z).
Axes of the slice: x: 2, y: 2, z: 4, core: 2. Of those that a mesh axis runs over, the one named last changes fastest.
Arguments:
- inputs: bfloat16 [4, 32, 8, 256], P('groups', 'space'), parts along dimension 0, may hold values from -6 to 6
- cotangent: bfloat16 [4, 32, 256], P('groups', 'space'), parts along dimension 0, may hold values from -6 to 6
- lift_weight: bfloat16 [8, 64], replicated, may hold values from -2 to 2
- lift_bias: float32 [64], replicated, may hold values from -3 to 3
- point_weight: bfloat16 [4, 64, 64], P('segment'), may hold values from -0.75 to 0.75
- layer_bias: float32 [4, 64], P('segment'), may hold values from -2 to 2
- spectral_weight: bfloat16 [4, 16, 32, 2, 64, 64], P('segment', 'space'), may hold values from -0.5 to 0.5
- proj_weight: bfloat16 [64, 128], replicated, may hold values from -0.75 to 0.75
- proj_bias: float32 [128], replicated, may hold values from -3 to 3
- out_weight: bfloat16 [128], replicated, may hold values from -0.5 to 0.5
Outputs:
- spectral_grad: float32 [8, 16, 32, 2, 64, 64], P(('groups', 'segment'), 'space'), parts along dimension 0
- point_grad: float32 [8, 64, 64], P(('groups', 'segment')), parts along dimension 0
The draws below stay inside these ranges and needn't reach their ends.
There are 2 independent parts, one for each index of `groups`. The reference program is written for one: setup_inputs(seed, part) draws one part's arguments, and reference() takes and returns one part's arrays. A program takes and returns all parts, laid end to end along the dimension named above; an argument that names none is the same for every part. Nothing has to cross between parts.
All inputs are finite; a program needn't handle non-finite values.
Results may differ from the reference program's by a relative error of at most 0.033.
Values may be sent and summed in bfloat16 or wider, within the bound.
A program may use at most 64 MiB of HBM per device.

```python
import math
from functools import partial
import jax
import jax.numpy as jnp
from jax import lax

C = 64
MODES = 16
CIN = 8
HID = 128
NY = 256
MB = 2
KX = 32
NX = 32
LAYERS = 4


def levels(stream_key, dims, cuts, low, top_value):
    loudness = 1.0
    for position, parts in cuts:
        heights = jax.random.uniform(jax.random.fold_in(jax.random.fold_in(stream_key, 6), position), (parts,), jnp.float32, low / len(cuts), top_value / len(cuts))
        loudness = loudness * jnp.repeat(jnp.exp(heights), dims[position] // parts).reshape((-1,) + (1,) * (len(dims) - 1 - position))
    return loudness


def gaussian(own_key, dims, deviation, bound, cuts=(), kind=jnp.bfloat16):
    entries = deviation * jax.random.normal(own_key, dims, jnp.float32)
    if cuts:
        entries = entries * levels(own_key, dims, cuts, -0.22, 0.18)
    return jnp.clip(entries, -bound, bound).astype(kind)


def setup_inputs(seed: int = 0, part: int = 0) -> dict:
    splits = jax.random.split(jax.random.key(seed), 11)
    part_splits = jax.random.split(jax.random.fold_in(splits[10], part), 11)
    return {
        "inputs": gaussian(part_splits[0], (MB, NX, CIN, NY), 1.0, 6.0, ((1, 4),)),
        "cotangent": gaussian(part_splits[1], (MB, NX, NY), 1.0, 6.0, ((1, 4),)),
        "lift_weight": gaussian(splits[2], (CIN, C), CIN ** -0.5, 2.0),
        "lift_bias": gaussian(splits[3], (C,), 0.5, 3.0, (), jnp.float32),
        "point_weight": gaussian(splits[4], (LAYERS, C, C), C ** -0.5, 0.75, ((0, 4),)),
        "layer_bias": gaussian(splits[5], (LAYERS, C), 0.3, 2.0, ((0, 4),), jnp.float32),
        "spectral_weight": gaussian(splits[6], (LAYERS, MODES, KX, 2, C, C), (2 * C) ** -0.5, 0.5, ((0, 4), (1, 4))),
        "proj_weight": gaussian(splits[7], (C, HID), C ** -0.5, 0.75),
        "proj_bias": gaussian(splits[8], (HID,), 0.5, 3.0, (), jnp.float32),
        "out_weight": gaussian(splits[9], (HID,), HID ** -0.5, 0.5),
    }


highest = lax.Precision.HIGHEST

def y_tables(col_count, mode_count):
    ycells = jnp.arange(col_count, dtype=jnp.int32)[:, None]
    ymodes = jnp.arange(mode_count, dtype=jnp.int32)[None, :]
    angles = (ycells * ymodes % col_count).astype(jnp.float32) * (2.0 * math.pi / col_count)
    factor = 1.0 / math.sqrt(col_count)
    forward = jnp.stack([jnp.cos(angles), -jnp.sin(angles)], axis=1) * factor
    doubled = jnp.where(ymodes == 0, 1.0, 2.0).astype(jnp.float32)
    inverse = jnp.stack([doubled * jnp.cos(angles), -doubled * jnp.sin(angles)], axis=0) * factor
    return (forward.astype(jnp.bfloat16), jnp.transpose(inverse, (0, 2, 1)).astype(jnp.bfloat16))

def x_tables(row_total, mode_count):
    kx_count = 2 * mode_count
    indices = jnp.arange(kx_count, dtype=jnp.int32)
    freq_values = jnp.where(indices < mode_count, indices, indices - kx_count)
    xcells = jnp.arange(row_total, dtype=jnp.int32)
    angles = (freq_values[:, None] * xcells[None, :] % row_total).astype(jnp.float32) * (2.0 * math.pi / row_total)
    factor = 1.0 / math.sqrt(row_total)
    cosine_part = jnp.cos(angles) * factor
    sine_part = jnp.sin(angles) * factor
    forward = jnp.stack([jnp.stack([cosine_part, sine_part], -1), jnp.stack([-sine_part, cosine_part], -1)], axis=1)
    cosine_flip = cosine_part.T
    sine_flip = sine_part.T
    inverse = jnp.stack([jnp.stack([cosine_flip, -sine_flip], -1), jnp.stack([sine_flip, cosine_flip], -1)], axis=1)
    return (forward, inverse)

def mode_mult(coeffs, kernel):
    real_in, imag_in = (coeffs[:, :, 0], coeffs[:, :, 1])
    real_kernel, imag_kernel = (kernel[:, :, 0], kernel[:, :, 1])
    product = partial(jnp.einsum, 'mjc,mjco->mjo', precision=highest)
    real_out = product(real_in, real_kernel) - product(imag_in, imag_kernel)
    imag_out = product(real_in, imag_kernel) + product(imag_in, real_kernel)
    return jnp.stack([real_out, imag_out], axis=2)

def mode_back(coeffs, mode_grads, kernel):
    real_in, imag_in = (coeffs[:, :, 0], coeffs[:, :, 1])
    real_grad, imag_grad = (mode_grads[:, :, 0], mode_grads[:, :, 1])
    real_kernel, imag_kernel = (kernel[:, :, 0], kernel[:, :, 1])
    outer_sum = partial(jnp.einsum, 'mjc,mjo->mjco', precision=highest)
    inner_sum = partial(jnp.einsum, 'mjo,mjco->mjc', precision=highest)
    kernel_real = outer_sum(real_in, real_grad) + outer_sum(imag_in, imag_grad)
    kernel_imag = outer_sum(real_in, imag_grad) - outer_sum(imag_in, real_grad)
    coeff_real = inner_sum(real_grad, real_kernel) + inner_sum(imag_grad, imag_kernel)
    coeff_imag = inner_sum(imag_grad, real_kernel) - inner_sum(real_grad, imag_kernel)
    return (jnp.stack([kernel_real, kernel_imag], axis=2), jnp.stack([coeff_real, coeff_imag], axis=2))

def gelu_grad(pre_act, upstream):
    _, pullback = jax.vjp(jax.nn.gelu, pre_act)
    return pullback(upstream)[0]

def reference(inputs, cotangent, lift_weight, lift_bias, point_weight, layer_bias, spectral_weight, proj_weight, proj_bias, out_weight):
    y_forward, y_inverse = y_tables(NY, MODES)
    x_forward, x_inverse = x_tables(NX, MODES)
    x_forward_adj = jnp.transpose(x_forward, (2, 3, 0, 1))
    x_inverse_adj = jnp.transpose(x_inverse, (2, 3, 0, 1))
    y_forward_wide = y_forward.astype(jnp.float32)
    y_inverse_wide = y_inverse.astype(jnp.float32)
    kernel_grads = [jnp.zeros((MODES, KX, 2, C, C), jnp.float32) for which_layer in range(LAYERS)]
    point_grads = [jnp.zeros((C, C), jnp.float32) for which_layer in range(LAYERS)]
    for which_batch in range(MB):
        sample = inputs[which_batch].astype(jnp.float32)
        activity = jnp.einsum('xty,tc->xcy', sample, lift_weight.astype(jnp.float32), precision=highest)
        activity = (activity + lift_bias[None, :, None]).astype(jnp.bfloat16)
        stored = []
        for which_layer in range(LAYERS):
            kernel = spectral_weight[which_layer].astype(jnp.float32)
            wide_act = activity.astype(jnp.float32)
            ycoef = jnp.einsum('xcy,ypm->xmpc', wide_act, y_forward_wide, precision=highest)
            coeffs = jnp.einsum('jqxp,xmpc->mjqc', x_forward, ycoef, precision=highest)
            spread = jnp.einsum('xpjq,mjqc->xmpc', x_inverse, mode_mult(coeffs, kernel), precision=highest)
            branch = jnp.einsum('xmpc,pmy->xcy', spread, y_inverse_wide, precision=highest)
            pointwise = jnp.einsum('xcy,co->xoy', wide_act, point_weight[which_layer].astype(jnp.float32), precision=highest)
            pre_act = pointwise + branch + layer_bias[which_layer][None, :, None]
            stored.append((activity, pre_act, coeffs))
            activity = jax.nn.gelu(pre_act).astype(jnp.bfloat16)
        hidden = jnp.einsum('xcy,ck->xky', activity.astype(jnp.float32), proj_weight.astype(jnp.float32), precision=highest)
        hidden = hidden + proj_bias[None, :, None]
        upstream = out_weight.astype(jnp.float32)[None, :, None] * cotangent[which_batch].astype(jnp.float32)[:, None, :]
        hidden_grad = gelu_grad(hidden, upstream).astype(jnp.bfloat16)
        grad_acts = jnp.einsum('xky,ck->xcy', hidden_grad.astype(jnp.float32), proj_weight.astype(jnp.float32), precision=highest).astype(jnp.bfloat16)
        for which_layer in reversed(range(LAYERS)):
            layer_in, pre_act, coeffs = stored[which_layer]
            kernel = spectral_weight[which_layer].astype(jnp.float32)
            pre_grad = gelu_grad(pre_act, grad_acts.astype(jnp.float32)).astype(jnp.bfloat16)
            pre_wide = pre_grad.astype(jnp.float32)
            point_grads[which_layer] = point_grads[which_layer] + jnp.einsum('xcy,xoy->co', layer_in.astype(jnp.float32), pre_wide, precision=highest)
            y_grads = jnp.einsum('xoy,pmy->xmpo', pre_wide, y_inverse_wide, precision=highest)
            mode_grads = jnp.einsum('jqxp,xmpo->mjqo', x_inverse_adj, y_grads, precision=highest)
            kernel_step, coeff_step = mode_back(coeffs, mode_grads, kernel)
            kernel_grads[which_layer] = kernel_grads[which_layer] + kernel_step
            back_rows = jnp.einsum('xpjq,mjqc->xmpc', x_forward_adj, coeff_step, precision=highest)
            back_branch = jnp.einsum('xmpc,ypm->xcy', back_rows, y_forward_wide, precision=highest)
            pointwise_back = jnp.einsum('co,xoy->xcy', point_weight[which_layer].astype(jnp.float32), pre_wide, precision=highest)
            grad_acts = (pointwise_back + back_branch).astype(jnp.bfloat16)
    factor = 1.0 / math.sqrt(MB * NX * NY)
    return (jnp.stack(kernel_grads), jnp.stack(point_grads) * factor)
```

```python
import functools
import math

import jax
import jax.numpy as jnp
import ml_dtypes
import numpy as np
from jax import lax
from jax.experimental import pallas as pl
from jax.experimental.pallas import tpu as pltpu
from jax.sharding import PartitionSpec as P

MESH = pl.DeviceIdType.MESH
F32 = jnp.float32
BF16 = jnp.bfloat16
VMEM_BYTES = 48 * 1024 * 1024


def dot(a, b, dims=((1,), (0,))):
    return lax.dot_general(a, b, (dims, ((), ())), preferred_element_type=F32)


def each(count, body):
    def step(i, carry):
        body(i)
        return carry

    lax.fori_loop(0, count, step, 0, unroll=count <= 64)


class Sizes:
    def __init__(self, batch, rows, cols, segments, spaces, owned, kx, channels):
        self.MB, self.rows, self.NY = batch, rows, cols
        self.L, self.S, self.own, self.J, self.C = segments, spaces, owned, kx, channels
        self.U = batch * rows // segments
        assert self.U * segments == batch * rows
        self.ML = 2 if owned % 2 == 0 and 2 * channels <= 128 else 1
        self.H = owned // self.ML
        self.RP = -(-self.U * self.H * 2 // 16) * 16
        self.LN = self.ML * channels
        self.RG = -(-self.ML * batch * 2 // 8) * 8
        self.N = segments * spaces
        self.K = self.N * self.RP
        self.R = self.H * kx * self.RG
        self.Y = self.U * cols


def make_tables(z):
    modes = z.own * z.S
    y = np.arange(z.NY)[:, None]
    m = np.arange(modes)[None, :]
    t = 2 * math.pi * ((y * m) % z.NY) / z.NY
    fy = np.stack([np.cos(t), -np.sin(t)], 1) / math.sqrt(z.NY)
    iy = fy * np.where(m == 0, 1.0, 2.0)[:, None, :]
    nx = z.rows * z.S
    f = np.arange(z.J)
    f = np.where(f < z.J // 2, f, f - z.J)
    u = 2 * math.pi * ((f[:, None] * np.arange(nx)[None, :]) % nx) / nx
    c, s = np.cos(u) / math.sqrt(nx), np.sin(u) / math.sqrt(nx)
    fx = np.stack([np.stack([c, s], -1), np.stack([-s, c], -1)], 1)
    ix = np.stack([np.stack([c.T, -s.T], -1), np.stack([s.T, c.T], -1)], 1)

    ytab = []
    for table in (fy, iy):
        out = np.zeros((z.ML, z.S, z.RP, z.U, z.NY))
        for ml in range(z.ML):
            for sp in range(z.S):
                for un in range(z.U):
                    for h in range(z.H):
                        for p in range(2):
                            mode = sp * z.own + h * z.ML + ml
                            out[ml, sp, (un * z.H + h) * 2 + p, un] = table[:, p, mode]
        ytab.append(out.reshape(z.ML * z.S * z.RP, z.Y))

    x1 = np.zeros((z.H, z.J, z.RG, z.N, z.RP))
    x2, xg = np.zeros_like(x1), np.zeros_like(x1)
    for g in range(z.L):
        for sp in range(z.S):
            for un in range(z.U):
                b, xl = divmod(g * z.U + un, z.rows)
                x = sp * z.rows + xl
                for h in range(z.H):
                    for p in range(2):
                        col = (un * z.H + h) * 2 + p
                        for ml in range(z.ML):
                            r = (ml * z.MB + b) * 2
                            at = g * z.S + sp
                            for q in range(2):
                                x1[h, :, r + q, at, col] = fx[:, q, x, p]
                                xg[h, :, r + q, at, col] = ix[x, p, :, q]
                            x2[h, :, r, at, col] = -fx[:, 1, x, p]
                            x2[h, :, r + 1, at, col] = fx[:, 0, x, p]
    xs = [a.reshape(z.R, z.K) for a in (x1, x2, xg)]
    tables = ytab + xs + [a.T for a in xs]
    return [np.ascontiguousarray(a).astype(ml_dtypes.bfloat16) for a in tables]


def gelu_parts(v):
    k = math.sqrt(2.0 / math.pi)
    v2 = v * v
    t = jnp.tanh(v * (k + (k * 0.044715) * v2))
    half = 0.5 + 0.5 * t
    return half, v2, t


def gelu_slope(v):
    k = math.sqrt(2.0 / math.pi)
    half, v2, t = gelu_parts(v)
    return half + (0.5 * v) * (1.0 - t * t) * (k + (3.0 * k * 0.044715) * v2)


def main_kernel(
    z, inputs, cotangent, lift_wt, lift_b, pack_own, weights, proj_w, proj_wt, proj_b, out_w,
    yf, yi, x1, x2, xg, x1t, x2t, xgt,
    zz_out, ll_out, pg_out,
    acts, slopes, pregrad, grad, pack, msg, recv, omsg, back, modes, spread, pgs, pgr,
    to_send, to_recv, back_send, back_recv, pg_send, pg_recv, gat_send, gat_recv,
):
    C, LN, Q = z.C, z.LN, z.MB * 2
    seg, sp = lax.axis_index("segment"), lax.axis_index("space")
    me = seg * z.S + sp
    barrier = pltpu.get_barrier_semaphore()

    def device(g, s):
        return {"segment": g, "space": s}

    def greet(i):
        @pl.when(i != me)
        def _():
            pl.semaphore_signal(
                barrier, inc=1, device_id=device(i // z.S, i % z.S), device_id_type=MESH
            )

    each(z.N, greet)

    def remote(src, dst, send, receive, g, s):
        return pltpu.make_async_remote_copy(
            src_ref=src, dst_ref=dst, send_sem=send, recv_sem=receive,
            device_id=device(g, s), device_id_type=MESH,
        )

    def to_copy(layer, s):
        return remote(msg.at[s], recv.at[me], to_send.at[s], to_recv.at[me], layer, s)

    def from_copy(src):
        return remote(
            msg.at[0], recv.at[src], to_send.at[0], to_recv.at[src], src // z.S, src % z.S
        )

    def back_copy(i):
        return remote(
            omsg.at[i], back.at[sp], back_send.at[i], back_recv.at[sp], i // z.S, i % z.S
        )

    def back_from(layer, s):
        return remote(omsg.at[0], back.at[s], back_send.at[0], back_recv.at[s], layer, s)

    def pg_copy(layer, s):
        return remote(pgs.at[layer], pgr.at[me], pg_send.at[s], pg_recv.at[me], layer, s)

    def pg_from(src):
        return remote(
            pgs.at[0], pgr.at[src], pg_send.at[0], pg_recv.at[src], src // z.S, src % z.S
        )

    def pack_copy(g):
        return remote(pack_own, pack.at[seg], gat_send.at[g], gat_recv.at[seg], g, sp)

    def pack_from(g):
        return remote(pack_own, pack.at[g], gat_send.at[g], gat_recv.at[g], g, sp)

    def other(g, s, act):
        pl.when(jnp.logical_not((seg == g) & (sp == s)))(act)

    def send_rows(layer, table, values, wait_layer):
        co = dot(table[...], values, ((1,), (1,)))
        part = z.S * z.RP
        wide = jnp.concatenate([co[i * part : (i + 1) * part] for i in range(z.ML)], axis=1)
        if wait_layer is not None:
            each(z.S, lambda s: other(wait_layer, s, lambda: to_copy(wait_layer, s).wait_send()))
        msg[...] = wide.astype(BF16).reshape(z.S, z.RP, LN)
        each(z.S, lambda s: other(layer, s, lambda: to_copy(layer, s).start()))

        @pl.when(seg == layer)
        def _():
            recv[me] = msg[sp]

    def received():
        each(z.N, lambda i: pl.when(i != me)(lambda: from_copy(i).wait_recv()))
        return recv[...].reshape(z.K, LN)

    def answer(rows):
        omsg[...] = rows.astype(BF16).reshape(z.N, z.RP, LN)
        each(z.N, lambda i: pl.when(i != me)(lambda: back_copy(i).start()))
        back[sp] = omsg[me]

    def answer_sent():
        each(z.N, lambda i: pl.when(i != me)(lambda: back_copy(i).wait_send()))

    def answered(layer):
        each(z.S, lambda s: other(layer, s, lambda: back_from(layer, s).wait_recv()))
        rows = back[...].reshape(z.S * z.RP, LN)
        return jnp.concatenate([rows[:, i * C : (i + 1) * C] for i in range(z.ML)], axis=0)

    def own_part(value):
        row = lax.broadcasted_iota(jnp.int32, value.shape, 0) % z.RG // Q
        lane = lax.broadcasted_iota(jnp.int32, value.shape, 1) // C
        return jnp.where(row == lane, value, 0.0)

    def kernel_of(i):
        h, j = i // z.J, i % z.J
        return jnp.concatenate(
            [weights[h * z.ML + ml, j, q] for q in range(2) for ml in range(z.ML)], axis=0
        )

    def group(i):
        start = i * z.RG
        return pl.ds(start if isinstance(start, int) else pl.multiple_of(start, z.RG), z.RG)

    tail = lax.broadcasted_iota(jnp.int32, (128 - C, z.Y), 0)
    tail = jnp.where(tail < 2, 1.0, 0.0).astype(BF16)
    for layer in range(z.L):
        acts[layer, C:128, :] = tail
    for u in range(z.U):
        value = dot(lift_wt[...], inputs[seg * z.U + u]) + lift_b[...]
        acts[0, 0:C, u * z.NY : (u + 1) * z.NY] = value.astype(BF16)

    pl.semaphore_wait(barrier, z.N - 1)
    send_rows(0, yf, acts[0, 0:C, :], None)
    each(z.L, lambda g: pl.when(g != seg)(lambda: pack_copy(g).start()))
    pack[seg] = pack_own[...]
    each(z.L, lambda g: pl.when(g != seg)(lambda: pack_from(g).wait_recv()))

    def forward(layer, carry):
        @pl.when(seg == layer)
        def _():
            got = received()
            zz_out[:, 0:LN] = own_part(dot(x1[...], got))
            zz_out[:, LN : 2 * LN] = own_part(dot(x2[...], got))

            def mult(i):
                modes[group(i), :] = dot(zz_out[group(i), :].astype(BF16), kernel_of(i))

            each(z.H * z.J, mult)
            product = modes[...]
            product = own_part(jnp.concatenate([product] * z.ML, axis=1))
            answer(dot(xgt[...], product.astype(BF16)))

        local = dot(pack[layer, 0], acts[layer])
        pre = local + dot(answered(layer), yi[...], ((0,), (0,)))
        half, _, _ = gelu_parts(pre)
        acts[layer + 1, 0:C, :] = (pre * half).astype(BF16)

        @pl.when(layer < z.L - 1)
        def _():
            send_rows(layer + 1, yf, acts[layer + 1, 0:C, :], layer)

        slopes[layer] = gelu_slope(pre)
        return carry

    lax.fori_loop(0, z.L, forward, 0)
    answer_sent()

    hidden = dot(proj_wt[...], acts[z.L, 0:C, :]) + proj_b[...]
    target = jnp.concatenate([cotangent[seg * z.U + u] for u in range(z.U)], axis=1)
    hidden_grad = (gelu_slope(hidden) * out_w[...] * target).astype(BF16)
    grad[...] = dot(proj_w[...], hidden_grad).astype(BF16)

    def backward(step, carry):
        layer = z.L - 1 - step
        pregrad[...] = (grad[...].astype(F32) * slopes[layer]).astype(BF16)
        send_rows(layer, yi, pregrad[...], jnp.minimum(layer + 1, z.L - 1))

        @pl.when(step > 0)
        def _():
            each(z.S, lambda s: other(layer + 1, s, lambda: pg_copy(layer + 1, s).wait_send()))

        pgs[layer] = dot(acts[layer, 0:C, :], pregrad[...], ((1,), (1,))).astype(BF16)
        each(z.S, lambda s: other(layer, s, lambda: pg_copy(layer, s).start()))

        @pl.when(seg == layer)
        def _():
            pgr[me] = pgs[layer]
            got = dot(xg[...], received())
            if z.ML > 1:
                row = lax.broadcasted_iota(jnp.int32, (z.R, C), 0) % z.RG // Q
                got = jnp.where(row == 0, got[:, 0:C], got[:, C : 2 * C])
            ll_out[...] = got

            @pl.when(layer > 0)
            def _():
                def mult(i):
                    spread[group(i), :] = dot(
                        ll_out[group(i), :].astype(BF16), kernel_of(i), ((1,), (1,))
                    )

                each(z.H * z.J, mult)
                first = own_part(spread[:, 0:LN]).astype(BF16)
                second = own_part(spread[:, LN : 2 * LN]).astype(BF16)
                answer(dot(x1t[...], first) + dot(x2t[...], second))

        @pl.when(layer > 0)
        def _():
            local = dot(pack[layer, 1][:, 0:C], pregrad[...])
            grad[...] = (local + dot(answered(layer), yf[...], ((0,), (0,)))).astype(BF16)

        return carry

    lax.fori_loop(0, z.L, backward, 0)

    each(z.N, lambda i: pl.when(i != me)(lambda: pg_from(i).wait_recv()))
    total = pgr[0].astype(F32)
    for i in range(1, z.N):
        total = total + pgr[i].astype(F32)
    pg_out[...] = total * (1.0 / math.sqrt(z.MB * z.rows * z.S * z.NY))

    each(z.S, lambda s: other(0, s, lambda: pg_copy(0, s).wait_send()))
    each(z.S, lambda s: other(0, s, lambda: to_copy(0, s).wait_send()))
    pl.when(seg > 0)(answer_sent)
    each(z.L, lambda g: pl.when(g != seg)(lambda: pack_copy(g).wait_send()))


def outer_kernel(z, count, zz, ll, out):
    turned = zz[...].T.astype(BF16)
    grads = ll[...]
    row = lax.broadcasted_iota(jnp.int32, grads.shape, 0) // z.RG
    for jj in range(count):
        part = jnp.where(row == jj, grads, 0.0).astype(BF16)
        value = dot(turned, part)
        for q in range(2):
            for ml in range(z.ML):
                at = (q * z.ML + ml) * z.C
                out[ml, jj, q] = value[at : at + z.C]


def on_device(
    inputs, cotangent, lift_weight, lift_bias, point_weight, layer_bias, spectral_weight,
    proj_weight, proj_bias, out_weight,
):
    batch, rows, steps, cols = inputs.shape
    _, owned, kx, _, C, _ = spectral_weight.shape
    z = Sizes(batch, rows, cols, lax.axis_size("segment"), lax.axis_size("space"), owned, kx, C)
    hid = proj_weight.shape[1]
    tables = [jnp.asarray(t) for t in make_tables(z)]

    w = point_weight[0]
    bias = layer_bias[0]
    high = bias.astype(BF16)
    low = (bias - high.astype(F32)).astype(BF16)
    gap = jnp.zeros((C, 128 - C - 2), BF16)
    pack = jnp.stack(
        [
            jnp.concatenate([w.T, high[:, None], low[:, None], gap], axis=1),
            jnp.concatenate([w, jnp.zeros((C, 128 - C), BF16)], axis=1),
        ]
    )
    args = [
        inputs.reshape(batch * rows, steps, cols),
        cotangent.astype(F32).reshape(batch * rows, 1, cols),
        lift_weight.T,
        lift_bias[:, None],
        pack,
        spectral_weight[0],
        proj_weight,
        proj_weight.T,
        proj_bias[:, None],
        out_weight.astype(F32)[:, None],
    ] + tables
    vmem = pl.BlockSpec(memory_space=pltpu.VMEM)
    dma = pltpu.SemaphoreType.DMA
    zz, ll, point = pl.pallas_call(
        functools.partial(main_kernel, z),
        out_shape=[
            jax.ShapeDtypeStruct((z.R, 2 * z.LN), F32),
            jax.ShapeDtypeStruct((z.R, C), F32),
            jax.ShapeDtypeStruct((C, C), F32),
        ],
        in_specs=[vmem] * len(args),
        out_specs=[vmem] * 3,
        scratch_shapes=[
            pltpu.VMEM((z.L + 1, 128, z.Y), BF16),
            pltpu.VMEM((z.L, C, z.Y), F32),
            pltpu.VMEM((C, z.Y), BF16),
            pltpu.VMEM((C, z.Y), BF16),
            pltpu.VMEM((z.L, 2, C, 128), BF16),
            pltpu.VMEM((z.S, z.RP, z.LN), BF16),
            pltpu.VMEM((z.N, z.RP, z.LN), BF16),
            pltpu.VMEM((z.N, z.RP, z.LN), BF16),
            pltpu.VMEM((z.S, z.RP, z.LN), BF16),
            pltpu.VMEM((z.R, C), F32),
            pltpu.VMEM((z.R, 2 * z.LN), F32),
            pltpu.VMEM((z.L, C, C), BF16),
            pltpu.VMEM((z.N, C, C), BF16),
            dma((z.S,)),
            dma((z.N,)),
            dma((z.N,)),
            dma((z.S,)),
            dma((z.S,)),
            dma((z.N,)),
            dma((z.L,)),
            dma((z.L,)),
        ],
        compiler_params=pltpu.CompilerParams(
            collective_id=0, has_side_effects=True, vmem_limit_bytes=VMEM_BYTES
        ),
        name="operator",
    )(*args)

    count = min(128 // z.RG, z.J)
    blocks = z.J // count
    grads = pl.pallas_call(
        functools.partial(outer_kernel, z, count),
        grid=(z.H, blocks),
        out_shape=jax.ShapeDtypeStruct((owned, kx, 2, C, C), F32),
        in_specs=[
            pl.BlockSpec((count * z.RG, 2 * z.LN), lambda h, j: (h * blocks + j, 0)),
            pl.BlockSpec((count * z.RG, C), lambda h, j: (h * blocks + j, 0)),
        ],
        out_specs=pl.BlockSpec((z.ML, count, 2, C, C), lambda h, j: (h, j, 0, 0, 0)),
        compiler_params=pltpu.CompilerParams(vmem_limit_bytes=VMEM_BYTES),
        name="outer",
    )(zz, ll)
    return grads[None], point[None]


def solution(mesh):
    in_specs = (
        P("groups", "space", None, None),
        P("groups", "space", None),
        P(),
        P(),
        P("segment", None, None),
        P("segment", None),
        P("segment", "space", None, None, None, None),
        P(),
        P(),
        P(),
    )
    out_specs = (
        P(("groups", "segment"), "space", None, None, None, None),
        P(("groups", "segment"), None, None),
    )
    return jax.shard_map(
        on_device, mesh=mesh, in_specs=in_specs, out_specs=out_specs, check_vma=False
    )
```

```python
import functools
import math

import jax
import jax.numpy as jnp
import ml_dtypes
import numpy as np
from jax import lax
from jax.experimental import pallas as pl
from jax.experimental.pallas import tpu as pltpu
from jax.sharding import PartitionSpec as P

MESH = pl.DeviceIdType.MESH
F32 = jnp.float32
BF16 = jnp.bfloat16
VMEM_BYTES = 63 * 1024 * 1024


def dot(a, b, dims=((1,), (0,))):
    return lax.dot_general(a, b, (dims, ((), ())), preferred_element_type=F32)


def each(count, body):
    def step(i, carry):
        body(i)
        return carry

    lax.fori_loop(0, count, step, 0, unroll=count <= 64)


class Sizes:
    def __init__(self, batch, rows, cols, segments, spaces, owned, kx, channels):
        self.MB, self.rows, self.NY = batch, rows, cols
        self.L, self.S, self.own, self.J, self.C = segments, spaces, owned, kx, channels
        self.U = batch * rows // segments
        assert self.U * segments == batch * rows
        self.ML = 2 if owned % 2 == 0 and 2 * channels <= 128 else 1
        self.H = owned // self.ML
        self.RP = -(-self.U * self.H * 2 // 16) * 16
        self.LN = self.ML * channels
        self.RG = -(-self.ML * batch * 2 // 8) * 8
        self.N = segments * spaces
        self.K = self.N * self.RP
        self.R = self.H * kx * self.RG
        self.Y = self.U * cols


def make_tables(z):
    modes = z.own * z.S
    y = np.arange(z.NY)[:, None]
    m = np.arange(modes)[None, :]
    t = 2 * math.pi * ((y * m) % z.NY) / z.NY
    fy = np.stack([np.cos(t), -np.sin(t)], 1) / math.sqrt(z.NY)
    iy = fy * np.where(m == 0, 1.0, 2.0)[:, None, :]
    nx = z.rows * z.S
    f = np.arange(z.J)
    f = np.where(f < z.J // 2, f, f - z.J)
    u = 2 * math.pi * ((f[:, None] * np.arange(nx)[None, :]) % nx) / nx
    c, s = np.cos(u) / math.sqrt(nx), np.sin(u) / math.sqrt(nx)
    fx = np.stack([np.stack([c, s], -1), np.stack([-s, c], -1)], 1)

    ytab = []
    for table in (fy, iy):
        out = np.zeros((z.ML, z.S, z.RP, z.U, z.NY))
        for ml in range(z.ML):
            for sp in range(z.S):
                for un in range(z.U):
                    for h in range(z.H):
                        for p in range(2):
                            mode = sp * z.own + h * z.ML + ml
                            out[ml, sp, (un * z.H + h) * 2 + p, un] = table[:, p, mode]
        ytab.append(out.reshape(z.ML * z.S * z.RP, z.Y))

    x1 = np.zeros((z.H, z.J, z.RG, z.N, z.RP))
    x2 = np.zeros_like(x1)
    for g in range(z.L):
        for sp in range(z.S):
            for un in range(z.U):
                b, xl = divmod(g * z.U + un, z.rows)
                x = sp * z.rows + xl
                for h in range(z.H):
                    for p in range(2):
                        col = (un * z.H + h) * 2 + p
                        for ml in range(z.ML):
                            r = (ml * z.MB + b) * 2
                            at = g * z.S + sp
                            for q in range(2):
                                x1[h, :, r + q, at, col] = fx[:, q, x, p]
                            x2[h, :, r, at, col] = -fx[:, 1, x, p]
                            x2[h, :, r + 1, at, col] = fx[:, 0, x, p]
    xs = [a.reshape(z.R, z.K) for a in (x1, x2)]
    tables = ytab + xs + [a.T for a in xs]
    return [np.ascontiguousarray(a).astype(ml_dtypes.bfloat16) for a in tables]


def gelu_parts(v):
    k = math.sqrt(2.0 / math.pi)
    v2 = v * v
    t = jnp.tanh(v * (k + (k * 0.044715) * v2))
    half = 0.5 + 0.5 * t
    return half, v2, t


def gelu_slope(v):
    k = math.sqrt(2.0 / math.pi)
    half, v2, t = gelu_parts(v)
    return half + (0.5 * v) * (1.0 - t * t) * (k + (3.0 * k * 0.044715) * v2)


def main_kernel(
    z, inputs_hbm, cotangent_hbm, lift_w_hbm, lift_b_hbm, point_hbm, bias_hbm, weights_hbm,
    proj_w_hbm, proj_b_hbm, out_w_hbm, yf_hbm, yi_hbm, x1_hbm, x2_hbm, x1t_hbm, x2t_hbm,
    zz_out, ll_out, pg_out,
    inputs, cotangent, lift_w, lift_b, point, bias, weights,
    proj_w, proj_b, out_w, yf, yi, x1, x2, x1t, x2t, targets, in_sem,
    acts, slopes, pregrad, grad, pack, msg, recv, omsg, back, modes, spread, pgs, pgr,
    to_send, to_recv, back_send, back_recv, pg_send, pg_recv, gat_send, gat_recv,
):
    C, LN, Q = z.C, z.LN, z.MB * 2
    seg, sp = lax.axis_index("segment"), lax.axis_index("space")
    me = seg * z.S + sp
    barrier = pltpu.get_barrier_semaphore()

    def device(g, s):
        return {"segment": g, "space": s}

    def greet(d):
        i = (me + 1 + d) % z.N
        pl.semaphore_signal(
            barrier, inc=1, device_id=device(i // z.S, i % z.S), device_id_type=MESH
        )

    each(z.N - 1, greet)

    def fetch(k, src, dst):
        copy = pltpu.make_async_copy(src, dst, in_sem.at[k])
        copy.start()
        return copy

    first = [(inputs_hbm, inputs), (lift_w_hbm, lift_w), (lift_b_hbm, lift_b), (yf_hbm, yf)]
    second = [(point_hbm, point), (bias_hbm, bias), (yi_hbm, yi), (cotangent_hbm, cotangent)]
    second += [(proj_w_hbm, proj_w), (proj_b_hbm, proj_b), (out_w_hbm, out_w)]
    third = [(x1_hbm, x1), (x2_hbm, x2), (weights_hbm, weights), (x1t_hbm, x1t), (x2t_hbm, x2t)]
    pairs = first + second + third
    copies = [fetch(k, src, dst) for k, (src, dst) in enumerate(pairs)]
    third_copies = copies[len(first) + len(second) :]

    def column(row):
        n = row.shape[1]
        eye = lax.broadcasted_iota(jnp.int32, (n, n), 0) == lax.broadcasted_iota(
            jnp.int32, (n, n), 1
        )
        return jnp.sum(jnp.where(eye, row, 0.0), axis=1, keepdims=True)

    def remote(src, dst, send, receive, g, s):
        return pltpu.make_async_remote_copy(
            src_ref=src, dst_ref=dst, send_sem=send, recv_sem=receive,
            device_id=device(g, s), device_id_type=MESH,
        )

    def to_copy(layer, s):
        return remote(msg.at[s], recv.at[me], to_send.at[s], to_recv.at[me], layer, s)

    def from_copy(src):
        return remote(
            msg.at[0], recv.at[src], to_send.at[0], to_recv.at[src], src // z.S, src % z.S
        )

    def back_copy(i):
        return remote(
            omsg.at[i], back.at[sp], back_send.at[i], back_recv.at[sp], i // z.S, i % z.S
        )

    def back_from(layer, s):
        return remote(omsg.at[0], back.at[s], back_send.at[0], back_recv.at[s], layer, s)

    def pg_copy(layer, s):
        return remote(pgs.at[layer], pgr.at[me], pg_send.at[s], pg_recv.at[me], layer, s)

    def pg_from(src):
        return remote(
            pgs.at[0], pgr.at[src], pg_send.at[0], pg_recv.at[src], src // z.S, src % z.S
        )

    def pack_copy(g):
        return remote(pack.at[seg], pack.at[seg], gat_send.at[g], gat_recv.at[seg], g, sp)

    def pack_from(g):
        return remote(pack.at[g], pack.at[g], gat_send.at[g], gat_recv.at[g], g, sp)

    def owners(g, act):
        pl.when(seg != g)(lambda: act(sp))
        each(z.S - 1, lambda d: act((sp + 1 + d) % z.S))

    def others(act):
        each(z.N - 1, lambda d: act((me + 1 + d) % z.N))

    def send_rows(layer, table, values, wait_layer):
        co = dot(table[...], values, ((1,), (1,)))
        part = z.S * z.RP
        wide = jnp.concatenate([co[i * part : (i + 1) * part] for i in range(z.ML)], axis=1)
        if wait_layer is not None:
            owners(wait_layer, lambda s: to_copy(wait_layer, s).wait_send())
        msg[...] = wide.astype(BF16).reshape(z.S, z.RP, LN)
        owners(layer, lambda s: to_copy(layer, s).start())

        @pl.when(seg == layer)
        def _():
            recv[me] = msg[sp]

    def received():
        others(lambda i: from_copy(i).wait_recv())
        return recv[...].reshape(z.K, LN)

    def answer(rows):
        omsg[...] = rows.astype(BF16).reshape(z.N, z.RP, LN)
        others(lambda i: back_copy(i).start())
        back[sp] = omsg[me]

    def answer_sent():
        others(lambda i: back_copy(i).wait_send())

    def answered(layer):
        owners(layer, lambda s: back_from(layer, s).wait_recv())
        rows = back[...].reshape(z.S * z.RP, LN)
        return jnp.concatenate([rows[:, i * C : (i + 1) * C] for i in range(z.ML)], axis=0)

    def own_part(value):
        row = lax.broadcasted_iota(jnp.int32, (z.RG, LN), 0) // Q
        lane = lax.broadcasted_iota(jnp.int32, (z.RG, LN), 1) // C
        grouped = value.reshape(z.R // z.RG, z.RG, LN)
        return jnp.where((row == lane)[None], grouped, 0.0).reshape(z.R, LN)

    def kernel_of(i):
        h, j = i // z.J, i % z.J
        return jnp.concatenate(
            [weights[h * z.ML + ml, j, q] for q in range(2) for ml in range(z.ML)], axis=0
        )

    def group(i):
        start = i * z.RG
        return pl.ds(start if isinstance(start, int) else pl.multiple_of(start, z.RG), z.RG)

    tail = lax.broadcasted_iota(jnp.int32, (128 - C, z.Y), 0)
    tail = jnp.where(tail < 2, 1.0, 0.0).astype(BF16)
    for layer in range(z.L):
        acts[layer, C:128, :] = tail
    for copy in copies[: len(first)]:
        copy.wait()
    shift = column(lift_b[...])
    for u in range(z.U):
        value = dot(lift_w[...], inputs[seg * z.U + u], ((0,), (0,))) + shift
        acts[0, 0:C, u * z.NY : (u + 1) * z.NY] = value.astype(BF16)

    pl.semaphore_wait(barrier, z.N - 1)
    send_rows(0, yf, acts[0, 0:C, :], None)

    for copy in copies[len(first) : len(first) + len(second)]:
        copy.wait()
    wide = point[...].astype(F32)
    high = bias[...].astype(BF16).astype(F32)
    lane = lax.broadcasted_iota(jnp.int32, (C, 128 - C), 1)
    side = jnp.where(lane == 0, column(high), jnp.where(lane == 1, column(bias[...] - high), 0.0))
    pack[seg, 0] = jnp.concatenate([wide.T, side], axis=1).astype(BF16)
    pack[seg, 1] = jnp.concatenate([wide, jnp.zeros_like(side)], axis=1).astype(BF16)
    each(z.L - 1, lambda d: pack_copy((seg + 1 + d) % z.L).start())
    targets[...] = cotangent[...].astype(F32).reshape(z.MB * z.rows, z.NY)
    each(z.L - 1, lambda d: pack_from((seg + 1 + d) % z.L).wait_recv())

    def forward(layer, carry):
        @pl.when(seg == layer)
        def _():
            for copy in third_copies:
                copy.wait()
            got = received()
            zz_out[:, 0:LN] = own_part(dot(x1[...], got))
            zz_out[:, LN : 2 * LN] = own_part(dot(x2[...], got))

            def mult(i):
                modes[group(i), :] = dot(zz_out[group(i), :].astype(BF16), kernel_of(i))

            each(z.H * z.J, mult)
            product = modes[...]
            product = own_part(jnp.concatenate([product] * z.ML, axis=1))
            answer(dot(x1t[...], product.astype(BF16)))

        local = dot(pack[layer, 0], acts[layer])
        pre = local + dot(answered(layer), yi[...], ((0,), (0,)))
        half, _, _ = gelu_parts(pre)
        acts[layer + 1, 0:C, :] = (pre * half).astype(BF16)

        @pl.when(layer < z.L - 1)
        def _():
            send_rows(layer + 1, yf, acts[layer + 1, 0:C, :], layer)

        slopes[layer] = gelu_slope(pre)
        return carry

    lax.fori_loop(0, z.L, forward, 0)
    answer_sent()

    hidden = dot(proj_w[...], acts[z.L, 0:C, :], ((0,), (0,))) + column(proj_b[...])
    target = jnp.concatenate([targets[pl.ds(seg * z.U + u, 1), :] for u in range(z.U)], axis=1)
    hidden_grad = (gelu_slope(hidden) * column(out_w[...]) * target).astype(BF16)
    grad[...] = dot(proj_w[...], hidden_grad).astype(BF16)

    def backward(step, carry):
        layer = z.L - 1 - step
        pregrad[...] = (grad[...].astype(F32) * slopes[layer]).astype(BF16)
        send_rows(layer, yi, pregrad[...], jnp.minimum(layer + 1, z.L - 1))

        @pl.when(step > 0)
        def _():
            owners(layer + 1, lambda s: pg_copy(layer + 1, s).wait_send())

        pgs[layer] = dot(acts[layer, 0:C, :], pregrad[...], ((1,), (1,))).astype(BF16)
        owners(layer, lambda s: pg_copy(layer, s).start())

        @pl.when(seg == layer)
        def _():
            pgr[me] = pgs[layer]
            got = dot(x1[...], received())
            if z.ML > 1:
                row = lax.broadcasted_iota(jnp.int32, (z.RG, C), 0) < Q
                halves = [a.reshape(z.R // z.RG, z.RG, C) for a in (got[:, 0:C], got[:, C : 2 * C])]
                got = jnp.where(row[None], halves[0], halves[1]).reshape(z.R, C)
            ll_out[...] = got

            @pl.when(layer > 0)
            def _():
                def mult(i):
                    spread[group(i), :] = dot(
                        ll_out[group(i), :].astype(BF16), kernel_of(i), ((1,), (1,))
                    )

                each(z.H * z.J, mult)
                first = own_part(spread[:, 0:LN]).astype(BF16)
                second = own_part(spread[:, LN : 2 * LN]).astype(BF16)
                answer(dot(x1t[...], first) + dot(x2t[...], second))

        @pl.when(layer > 0)
        def _():
            local = dot(pack[layer, 1][:, 0:C], pregrad[...])
            grad[...] = (local + dot(answered(layer), yf[...], ((0,), (0,)))).astype(BF16)

        return carry

    lax.fori_loop(0, z.L, backward, 0)

    others(lambda i: pg_from(i).wait_recv())
    total = pgr[0].astype(F32)
    for i in range(1, z.N):
        total = total + pgr[i].astype(F32)
    pg_out[...] = total * (1.0 / math.sqrt(z.MB * z.rows * z.S * z.NY))

    owners(0, lambda s: pg_copy(0, s).wait_send())
    owners(0, lambda s: to_copy(0, s).wait_send())
    pl.when(seg > 0)(answer_sent)
    each(z.L - 1, lambda d: pack_copy((seg + 1 + d) % z.L).wait_send())


def outer_kernel(z, count, zz, ll, point, out, point_out):
    point_out[...] = point[...]
    turned = zz[...].T.astype(BF16)
    grads = ll[...]
    row = lax.broadcasted_iota(jnp.int32, grads.shape, 0) // z.RG
    for jj in range(count):
        part = jnp.where(row == jj, grads, 0.0).astype(BF16)
        value = dot(turned, part)
        for q in range(2):
            for ml in range(z.ML):
                at = (q * z.ML + ml) * z.C
                out[ml, jj, q] = value[at : at + z.C]


def on_device(
    inputs, cotangent, lift_weight, lift_bias, point_weight, layer_bias, spectral_weight,
    proj_weight, proj_bias, out_weight,
):
    batch, rows, steps, cols = inputs.shape
    _, owned, kx, _, C, _ = spectral_weight.shape
    z = Sizes(batch, rows, cols, lax.axis_size("segment"), lax.axis_size("space"), owned, kx, C)
    tables = [jnp.asarray(t) for t in make_tables(z)]

    args = [
        inputs.reshape(batch * rows, steps, cols),
        cotangent,
        lift_weight,
        lift_bias[None],
        point_weight[0],
        layer_bias,
        spectral_weight[0],
        proj_weight,
        proj_bias[None],
        out_weight.astype(F32)[None],
    ] + tables
    held = [pltpu.VMEM(a.shape, a.dtype) for a in args]
    vmem = pl.BlockSpec(memory_space=pltpu.VMEM)
    dma = pltpu.SemaphoreType.DMA
    zz, ll, point = pl.pallas_call(
        functools.partial(main_kernel, z),
        out_shape=[
            jax.ShapeDtypeStruct((z.R, 2 * z.LN), F32),
            jax.ShapeDtypeStruct((z.R, C), F32),
            jax.ShapeDtypeStruct((C, C), F32),
        ],
        in_specs=[pl.BlockSpec(memory_space=pltpu.HBM)] * len(args),
        out_specs=[vmem] * 3,
        scratch_shapes=held
        + [
            pltpu.VMEM((batch * rows, cols), F32),
            dma((len(args),)),
            pltpu.VMEM((z.L + 1, 128, z.Y), BF16),
            pltpu.VMEM((z.L, C, z.Y), F32),
            pltpu.VMEM((C, z.Y), BF16),
            pltpu.VMEM((C, z.Y), BF16),
            pltpu.VMEM((z.L, 2, C, 128), BF16),
            pltpu.VMEM((z.S, z.RP, z.LN), BF16),
            pltpu.VMEM((z.N, z.RP, z.LN), BF16),
            pltpu.VMEM((z.N, z.RP, z.LN), BF16),
            pltpu.VMEM((z.S, z.RP, z.LN), BF16),
            pltpu.VMEM((z.R, C), F32),
            pltpu.VMEM((z.R, 2 * z.LN), F32),
            pltpu.VMEM((z.L, C, C), BF16),
            pltpu.VMEM((z.N, C, C), BF16),
            dma((z.S,)),
            dma((z.N,)),
            dma((z.N,)),
            dma((z.S,)),
            dma((z.S,)),
            dma((z.N,)),
            dma((z.L,)),
            dma((z.L,)),
        ],
        compiler_params=pltpu.CompilerParams(
            collective_id=0, has_side_effects=True, vmem_limit_bytes=VMEM_BYTES
        ),
        name="operator",
    )(*args)

    count = min(64 // z.RG, z.J)
    blocks = z.J // count
    grads, point = pl.pallas_call(
        functools.partial(outer_kernel, z, count),
        grid=(z.H, blocks),
        out_shape=[
            jax.ShapeDtypeStruct((owned, kx, 2, C, C), F32),
            jax.ShapeDtypeStruct((C, C), F32),
        ],
        in_specs=[
            pl.BlockSpec((count * z.RG, 2 * z.LN), lambda h, j: (h * blocks + j, 0)),
            pl.BlockSpec((count * z.RG, C), lambda h, j: (h * blocks + j, 0)),
            pl.BlockSpec((C, C), lambda h, j: (0, 0)),
        ],
        out_specs=[
            pl.BlockSpec((z.ML, count, 2, C, C), lambda h, j: (h, j, 0, 0, 0)),
            pl.BlockSpec((C, C), lambda h, j: (0, 0)),
        ],
        compiler_params=pltpu.CompilerParams(vmem_limit_bytes=VMEM_BYTES),
        name="outer",
    )(zz, ll, point)
    return grads[None], point[None]


def solution(mesh):
    in_specs = (
        P("groups", "space", None, None),
        P("groups", "space", None),
        P(),
        P(),
        P("segment", None, None),
        P("segment", None),
        P("segment", "space", None, None, None, None),
        P(),
        P(),
        P(),
    )
    out_specs = (
        P(("groups", "segment"), "space", None, None, None, None),
        P(("groups", "segment"), None, None),
    )
    return jax.shard_map(
        on_device, mesh=mesh, in_specs=in_specs, out_specs=out_specs, check_vma=False
    )
```

```python
import functools
import math

import jax
import jax.numpy as jnp
import ml_dtypes
import numpy as np
from jax import lax
from jax.experimental import pallas as pl
from jax.experimental.pallas import tpu as pltpu
from jax.sharding import PartitionSpec as P

MESH = pl.DeviceIdType.MESH
F32 = jnp.float32
BF16 = jnp.bfloat16
VMEM_BYTES = 63 * 1024 * 1024


def dot(a, b, dims=((1,), (0,))):
    return lax.dot_general(a, b, (dims, ((), ())), preferred_element_type=F32)


def each(count, body):
    def step(i, carry):
        body(i)
        return carry

    lax.fori_loop(0, count, step, 0, unroll=count <= 64)


class Sizes:
    def __init__(self, batch, rows, cols, segments, spaces, owned, kx, channels):
        self.MB, self.rows, self.NY = batch, rows, cols
        self.L, self.S, self.own, self.J, self.C = segments, spaces, owned, kx, channels
        self.U = batch * rows // segments
        assert self.U * segments == batch * rows
        self.ML = 2 if owned % 2 == 0 and 2 * channels <= 128 else 1
        self.H = owned // self.ML
        self.RP = -(-self.U * self.H * 2 // 16) * 16
        self.LN = self.ML * channels
        self.RG = -(-self.ML * batch * 2 // 8) * 8
        self.N = segments * spaces
        self.K = self.N * self.RP
        self.R = self.H * kx * self.RG
        self.Y = self.U * cols


def make_tables(z):
    modes = z.own * z.S
    y = np.arange(z.NY)[:, None]
    m = np.arange(modes)[None, :]
    t = 2 * math.pi * ((y * m) % z.NY) / z.NY
    fy = np.stack([np.cos(t), -np.sin(t)], 1) / math.sqrt(z.NY)
    iy = fy * np.where(m == 0, 1.0, 2.0)[:, None, :]
    nx = z.rows * z.S
    f = np.arange(z.J)
    f = np.where(f < z.J // 2, f, f - z.J)
    u = 2 * math.pi * ((f[:, None] * np.arange(nx)[None, :]) % nx) / nx
    c, s = np.cos(u) / math.sqrt(nx), np.sin(u) / math.sqrt(nx)
    fx = np.stack([np.stack([c, s], -1), np.stack([-s, c], -1)], 1)

    ytab = []
    for table in (fy, iy):
        out = np.zeros((z.ML, z.S, z.RP, z.U, z.NY))
        for ml in range(z.ML):
            for sp in range(z.S):
                for un in range(z.U):
                    for h in range(z.H):
                        for p in range(2):
                            mode = sp * z.own + h * z.ML + ml
                            out[ml, sp, (un * z.H + h) * 2 + p, un] = table[:, p, mode]
        ytab.append(out.reshape(z.ML * z.S * z.RP, z.Y))

    x1 = np.zeros((z.H, z.J, z.RG, z.N, z.RP))
    x2 = np.zeros_like(x1)
    for g in range(z.L):
        for sp in range(z.S):
            for un in range(z.U):
                b, xl = divmod(g * z.U + un, z.rows)
                x = sp * z.rows + xl
                for h in range(z.H):
                    for p in range(2):
                        col = (un * z.H + h) * 2 + p
                        for ml in range(z.ML):
                            r = (ml * z.MB + b) * 2
                            at = g * z.S + sp
                            for q in range(2):
                                x1[h, :, r + q, at, col] = fx[:, q, x, p]
                            x2[h, :, r, at, col] = -fx[:, 1, x, p]
                            x2[h, :, r + 1, at, col] = fx[:, 0, x, p]
    xs = [a.reshape(z.R, z.K) for a in (x1, x2)]
    tables = ytab + xs + [a.T for a in xs]
    return [np.ascontiguousarray(a).astype(ml_dtypes.bfloat16) for a in tables]


def gelu_parts(v):
    k = math.sqrt(2.0 / math.pi)
    v2 = v * v
    t = jnp.tanh(v * (k + (k * 0.044715) * v2))
    half = 0.5 + 0.5 * t
    return half, v2, t


def gelu_slope(v):
    k = math.sqrt(2.0 / math.pi)
    half, v2, t = gelu_parts(v)
    return half + (0.5 * v) * (1.0 - t * t) * (k + (3.0 * k * 0.044715) * v2)


def main_kernel(
    z, inputs_hbm, cotangent_hbm, lift_w_hbm, lift_b_hbm, point_hbm, bias_hbm, weights_hbm,
    proj_w_hbm, proj_b_hbm, out_w_hbm, yf_hbm, yi_hbm, x1_hbm, x2_hbm, x1t_hbm, x2t_hbm,
    zz_out, ll_out, pg_out,
    inputs, cotangent, lift_w, lift_b, point, bias, weights,
    proj_w, proj_b, out_w, yf, yi, x1, x2, x1t, x2t, targets, in_sem,
    acts, slopes, pregrad, grad, pack, msg, recv, omsg, back, modes, spread, pgs, pgr,
    to_send, to_recv, back_send, back_recv, pg_send, pg_recv, gat_send, gat_recv,
):
    C, LN, Q = z.C, z.LN, z.MB * 2
    seg, sp = lax.axis_index("segment"), lax.axis_index("space")
    me = seg * z.S + sp
    barrier = pltpu.get_barrier_semaphore()

    def device(g, s):
        return {"segment": g, "space": s}

    def greet(d):
        i = (me + 1 + d) % z.N
        pl.semaphore_signal(
            barrier, inc=1, device_id=device(i // z.S, i % z.S), device_id_type=MESH
        )

    def fetch(k, src, dst):
        copy = pltpu.make_async_copy(src, dst, in_sem.at[k])
        copy.start()
        return copy

    first = [(inputs_hbm, inputs), (lift_w_hbm, lift_w), (lift_b_hbm, lift_b), (yf_hbm, yf)]
    second = [(point_hbm, point), (bias_hbm, bias), (yi_hbm, yi), (cotangent_hbm, cotangent)]
    second += [(proj_w_hbm, proj_w), (proj_b_hbm, proj_b), (out_w_hbm, out_w)]
    third = [(x1_hbm, x1), (x2_hbm, x2), (weights_hbm, weights), (x1t_hbm, x1t), (x2t_hbm, x2t)]
    pairs = first + second + third
    copies = [fetch(k, src, dst) for k, (src, dst) in enumerate(pairs)]
    each(z.N - 1, greet)
    third_copies = copies[len(first) + len(second) :]

    def column(row):
        n = row.shape[1]
        eye = lax.broadcasted_iota(jnp.int32, (n, n), 0) == lax.broadcasted_iota(
            jnp.int32, (n, n), 1
        )
        return jnp.sum(jnp.where(eye, row, 0.0), axis=1, keepdims=True)

    def remote(src, dst, send, receive, g, s):
        return pltpu.make_async_remote_copy(
            src_ref=src, dst_ref=dst, send_sem=send, recv_sem=receive,
            device_id=device(g, s), device_id_type=MESH,
        )

    def to_copy(layer, s):
        return remote(msg.at[s], recv.at[me], to_send.at[s], to_recv.at[me], layer, s)

    def from_copy(src):
        return remote(
            msg.at[0], recv.at[src], to_send.at[0], to_recv.at[src], src // z.S, src % z.S
        )

    def back_copy(i):
        return remote(
            omsg.at[i], back.at[sp], back_send.at[i], back_recv.at[sp], i // z.S, i % z.S
        )

    def back_from(layer, s):
        return remote(omsg.at[0], back.at[s], back_send.at[0], back_recv.at[s], layer, s)

    def pg_copy(layer, s):
        return remote(pgs.at[layer], pgr.at[me], pg_send.at[s], pg_recv.at[me], layer, s)

    def pg_from(src):
        return remote(
            pgs.at[0], pgr.at[src], pg_send.at[0], pg_recv.at[src], src // z.S, src % z.S
        )

    def pack_copy(g):
        return remote(pack.at[seg], pack.at[seg], gat_send.at[g], gat_recv.at[seg], g, sp)

    def pack_from(g):
        return remote(pack.at[g], pack.at[g], gat_send.at[g], gat_recv.at[g], g, sp)

    def owners(g, act):
        pl.when(seg != g)(lambda: act(sp))
        each(z.S - 1, lambda d: act((sp + 1 + d) % z.S))

    def others(act):
        each(z.N - 1, lambda d: act((me + 1 + d) % z.N))

    def send_rows(layer, table, values, wait_layer):
        co = dot(table[...], values, ((1,), (1,)))
        part = z.S * z.RP
        wide = jnp.concatenate([co[i * part : (i + 1) * part] for i in range(z.ML)], axis=1)
        if wait_layer is not None:
            owners(wait_layer, lambda s: to_copy(wait_layer, s).wait_send())
        msg[...] = wide.astype(BF16).reshape(z.S, z.RP, LN)
        owners(layer, lambda s: to_copy(layer, s).start())

        @pl.when(seg == layer)
        def _():
            recv[me] = msg[sp]

    def received():
        others(lambda i: from_copy(i).wait_recv())
        return recv[...].reshape(z.K, LN)

    def answer(rows):
        omsg[...] = rows.astype(BF16).reshape(z.N, z.RP, LN)
        others(lambda i: back_copy(i).start())
        back[sp] = omsg[me]

    def answer_sent():
        others(lambda i: back_copy(i).wait_send())

    def answered(layer):
        owners(layer, lambda s: back_from(layer, s).wait_recv())
        rows = back[...].reshape(z.S * z.RP, LN)
        return jnp.concatenate([rows[:, i * C : (i + 1) * C] for i in range(z.ML)], axis=0)

    def own_part(value):
        row = lax.broadcasted_iota(jnp.int32, (z.RG, LN), 0) // Q
        lane = lax.broadcasted_iota(jnp.int32, (z.RG, LN), 1) // C
        grouped = value.reshape(z.R // z.RG, z.RG, LN)
        return jnp.where((row == lane)[None], grouped, 0.0).reshape(z.R, LN)

    def kernel_of(i):
        h, j = i // z.J, i % z.J
        return jnp.concatenate(
            [weights[h * z.ML + ml, j, q] for q in range(2) for ml in range(z.ML)], axis=0
        )

    def group(i):
        start = i * z.RG
        return pl.ds(start if isinstance(start, int) else pl.multiple_of(start, z.RG), z.RG)

    tail = lax.broadcasted_iota(jnp.int32, (128 - C, z.Y), 0)
    tail = jnp.where(tail < 2, 1.0, 0.0).astype(BF16)
    for layer in range(z.L):
        acts[layer, C:128, :] = tail
    for copy in copies[: len(first)]:
        copy.wait()
    shift = column(lift_b[...])
    for u in range(z.U):
        value = dot(lift_w[...], inputs[seg * z.U + u], ((0,), (0,))) + shift
        acts[0, 0:C, u * z.NY : (u + 1) * z.NY] = value.astype(BF16)

    pl.semaphore_wait(barrier, z.N - 1)
    send_rows(0, yf, acts[0, 0:C, :], None)

    for copy in copies[len(first) : len(first) + len(second)]:
        copy.wait()
    wide = point[...].astype(F32)
    high = bias[...].astype(BF16).astype(F32)
    lane = lax.broadcasted_iota(jnp.int32, (C, 128 - C), 1)
    side = jnp.where(lane == 0, column(high), jnp.where(lane == 1, column(bias[...] - high), 0.0))
    pack[seg, 0] = jnp.concatenate([wide.T, side], axis=1).astype(BF16)
    pack[seg, 1] = jnp.concatenate([wide, jnp.zeros_like(side)], axis=1).astype(BF16)
    each(z.L - 1, lambda d: pack_copy((seg + 1 + d) % z.L).start())
    targets[...] = cotangent[...].astype(F32).reshape(z.MB * z.rows, z.NY)
    each(z.L - 1, lambda d: pack_from((seg + 1 + d) % z.L).wait_recv())

    def forward(layer, carry):
        @pl.when(seg == layer)
        def _():
            for copy in third_copies:
                copy.wait()
            got = received()
            zz_out[:, 0:LN] = own_part(dot(x1[...], got))
            zz_out[:, LN : 2 * LN] = own_part(dot(x2[...], got))

            def mult(i):
                modes[group(i), :] = dot(zz_out[group(i), :].astype(BF16), kernel_of(i))

            each(z.H * z.J, mult)
            product = modes[...]
            product = own_part(jnp.concatenate([product] * z.ML, axis=1))
            answer(dot(x1t[...], product.astype(BF16)))

        local = dot(pack[layer, 0], acts[layer])
        pre = local + dot(answered(layer), yi[...], ((0,), (0,)))
        half, _, _ = gelu_parts(pre)
        acts[layer + 1, 0:C, :] = (pre * half).astype(BF16)

        @pl.when(layer < z.L - 1)
        def _():
            send_rows(layer + 1, yf, acts[layer + 1, 0:C, :], layer)

        slopes[layer] = gelu_slope(pre)
        return carry

    lax.fori_loop(0, z.L, forward, 0)
    answer_sent()

    hidden = dot(proj_w[...], acts[z.L, 0:C, :], ((0,), (0,))) + column(proj_b[...])
    target = jnp.concatenate([targets[pl.ds(seg * z.U + u, 1), :] for u in range(z.U)], axis=1)
    hidden_grad = (gelu_slope(hidden) * column(out_w[...].astype(F32)) * target).astype(BF16)
    grad[...] = dot(proj_w[...], hidden_grad).astype(BF16)

    def backward(step, carry):
        layer = z.L - 1 - step
        pregrad[...] = (grad[...].astype(F32) * slopes[layer]).astype(BF16)
        send_rows(layer, yi, pregrad[...], jnp.minimum(layer + 1, z.L - 1))

        @pl.when(step > 0)
        def _():
            owners(layer + 1, lambda s: pg_copy(layer + 1, s).wait_send())

        pgs[layer] = dot(acts[layer, 0:C, :], pregrad[...], ((1,), (1,))).astype(BF16)
        owners(layer, lambda s: pg_copy(layer, s).start())

        @pl.when(seg == layer)
        def _():
            pgr[me] = pgs[layer]
            got = dot(x1[...], received())
            if z.ML > 1:
                row = lax.broadcasted_iota(jnp.int32, (z.RG, C), 0) < Q
                halves = [a.reshape(z.R // z.RG, z.RG, C) for a in (got[:, 0:C], got[:, C : 2 * C])]
                got = jnp.where(row[None], halves[0], halves[1]).reshape(z.R, C)
            ll_out[...] = got

            @pl.when(layer > 0)
            def _():
                def mult(i):
                    spread[group(i), :] = dot(
                        ll_out[group(i), :].astype(BF16), kernel_of(i), ((1,), (1,))
                    )

                each(z.H * z.J, mult)
                first = own_part(spread[:, 0:LN]).astype(BF16)
                second = own_part(spread[:, LN : 2 * LN]).astype(BF16)
                answer(dot(x1t[...], first) + dot(x2t[...], second))

        @pl.when(layer > 0)
        def _():
            local = dot(pack[layer, 1][:, 0:C], pregrad[...])
            grad[...] = (local + dot(answered(layer), yf[...], ((0,), (0,)))).astype(BF16)

        return carry

    lax.fori_loop(0, z.L, backward, 0)

    others(lambda i: pg_from(i).wait_recv())
    total = pgr[0].astype(F32)
    for i in range(1, z.N):
        total = total + pgr[i].astype(F32)
    pg_out[...] = total * (1.0 / math.sqrt(z.MB * z.rows * z.S * z.NY))

    owners(0, lambda s: pg_copy(0, s).wait_send())
    owners(0, lambda s: to_copy(0, s).wait_send())
    pl.when(seg > 0)(answer_sent)
    each(z.L - 1, lambda d: pack_copy((seg + 1 + d) % z.L).wait_send())


def outer_kernel(z, count, zz, ll, point, out, point_out):
    point_out[...] = point[...]
    turned = zz[...].T.astype(BF16)
    grads = ll[...]
    row = lax.broadcasted_iota(jnp.int32, grads.shape, 0) // z.RG
    for jj in range(count):
        part = jnp.where(row == jj, grads, 0.0).astype(BF16)
        value = dot(turned, part)
        for q in range(2):
            for ml in range(z.ML):
                at = (q * z.ML + ml) * z.C
                out[ml, jj, q] = value[at : at + z.C]


def on_device(
    inputs, cotangent, lift_weight, lift_bias, point_weight, layer_bias, spectral_weight,
    proj_weight, proj_bias, out_weight,
):
    batch, rows, steps, cols = inputs.shape
    _, owned, kx, _, C, _ = spectral_weight.shape
    z = Sizes(batch, rows, cols, lax.axis_size("segment"), lax.axis_size("space"), owned, kx, C)
    tables = [jnp.asarray(t) for t in make_tables(z)]

    args = [
        inputs.reshape(batch * rows, steps, cols),
        cotangent,
        lift_weight,
        lift_bias[None],
        point_weight[0],
        layer_bias,
        spectral_weight[0],
        proj_weight,
        proj_bias[None],
        out_weight[None],
    ] + tables
    held = [pltpu.VMEM(a.shape, a.dtype) for a in args]
    vmem = pl.BlockSpec(memory_space=pltpu.VMEM)
    dma = pltpu.SemaphoreType.DMA
    zz, ll, point = pl.pallas_call(
        functools.partial(main_kernel, z),
        out_shape=[
            jax.ShapeDtypeStruct((z.R, 2 * z.LN), F32),
            jax.ShapeDtypeStruct((z.R, C), F32),
            jax.ShapeDtypeStruct((C, C), F32),
        ],
        in_specs=[pl.BlockSpec(memory_space=pltpu.HBM)] * len(args),
        out_specs=[vmem] * 3,
        scratch_shapes=held
        + [
            pltpu.VMEM((batch * rows, cols), F32),
            dma((len(args),)),
            pltpu.VMEM((z.L + 1, 128, z.Y), BF16),
            pltpu.VMEM((z.L, C, z.Y), F32),
            pltpu.VMEM((C, z.Y), BF16),
            pltpu.VMEM((C, z.Y), BF16),
            pltpu.VMEM((z.L, 2, C, 128), BF16),
            pltpu.VMEM((z.S, z.RP, z.LN), BF16),
            pltpu.VMEM((z.N, z.RP, z.LN), BF16),
            pltpu.VMEM((z.N, z.RP, z.LN), BF16),
            pltpu.VMEM((z.S, z.RP, z.LN), BF16),
            pltpu.VMEM((z.R, C), F32),
            pltpu.VMEM((z.R, 2 * z.LN), F32),
            pltpu.VMEM((z.L, C, C), BF16),
            pltpu.VMEM((z.N, C, C), BF16),
            dma((z.S,)),
            dma((z.N,)),
            dma((z.N,)),
            dma((z.S,)),
            dma((z.S,)),
            dma((z.N,)),
            dma((z.L,)),
            dma((z.L,)),
        ],
        compiler_params=pltpu.CompilerParams(
            collective_id=0, has_side_effects=True, vmem_limit_bytes=VMEM_BYTES
        ),
        name="operator",
    )(*args)

    count = min(128 // z.RG, z.J)
    blocks = z.J // count
    grads, point = pl.pallas_call(
        functools.partial(outer_kernel, z, count),
        grid=(z.H, blocks),
        out_shape=[
            jax.ShapeDtypeStruct((owned, kx, 2, C, C), F32),
            jax.ShapeDtypeStruct((C, C), F32),
        ],
        in_specs=[
            pl.BlockSpec((count * z.RG, 2 * z.LN), lambda h, j: (h * blocks + j, 0)),
            pl.BlockSpec((count * z.RG, C), lambda h, j: (h * blocks + j, 0)),
            pl.BlockSpec((C, C), lambda h, j: (0, 0)),
        ],
        out_specs=[
            pl.BlockSpec((z.ML, count, 2, C, C), lambda h, j: (h, j, 0, 0, 0)),
            pl.BlockSpec((C, C), lambda h, j: (0, 0)),
        ],
        compiler_params=pltpu.CompilerParams(vmem_limit_bytes=VMEM_BYTES),
        name="outer",
    )(zz, ll, point)
    return grads[None], point[None]


def solution(mesh):
    in_specs = (
        P("groups", "space", None, None),
        P("groups", "space", None),
        P(),
        P(),
        P("segment", None, None),
        P("segment", None),
        P("segment", "space", None, None, None, None),
        P(),
        P(),
        P(),
    )
    out_specs = (
        P(("groups", "segment"), "space", None, None, None, None),
        P(("groups", "segment"), None, None),
    )
    return jax.shard_map(
        on_device, mesh=mesh, in_specs=in_specs, out_specs=out_specs, check_vma=False
    )
```
